32 devices in a mesh: dom: 32 (over z, y, x, core).
Axes of the slice: x: 2, y: 2, z: 4, core: 2. Of those that a mesh axis runs over, the one named last changes fastest.
Arguments:
- features: bfloat16 [16384, 768], P('dom'), may hold values from -6 to 6
- w_self: bfloat16 [768, 1024], replicated, may hold values from -0.21875 to 0.21875
- w_neigh: bfloat16 [768, 1024], replicated, may hold values from -0.21875 to 0.21875
- tile_cols: int32 [128, 6], P('dom'), may hold values from 0 to 6
- tile_weights: int32 [128, 6, 128, 128], P('dom'), may hold values from 0 to 3
- send_rows: int32 [32, 32, 32], P('dom'), may hold values from 0 to 511
- send_counts: int32 [32, 32], P('dom'), may hold values from 0 to 32, as said below
- hub_rows: int32 [32, 4], P('dom'), may hold values from 0 to 511
- readers: int32 [32, 128], P('dom'), may hold values 0 or 1
- cotangent: bfloat16 [16384, 1024], P('dom'), may hold values from -6 to 6
Outputs:
- out_rows: bfloat16 [16384, 1024], P('dom')
- grad_features: bfloat16 [16384, 768], P('dom')
- grad_self: float32 [768, 1024], replicated
- grad_neigh: float32 [768, 1024], replicated
The draws below stay inside these ranges and needn't reach their ends.
Inputs may be any that keep to these rules, and one draw needn't show every extreme that they name: send_counts[s, p] is the number of live leading slots of send_rows[s, p]; it is 0 for p == s and wherever (p - s) modulo 32 is neither within 1 to 4 nor within 28 to 31; for every s, send_counts[s, (s + 1) modulo 32] equals 32.
All inputs are finite; a program needn't handle non-finite values. No bound on the sum of `readers` on one device may be relied on, other than what follows from the above.
Results may differ from the reference program's by a relative error of at most 0.0054.
Values may be sent and summed in bfloat16 or wider, within the bound.
A program may use at most 192 MiB of HBM per device.

```python
import jax
import jax.numpy as jnp
from jax import lax

F = 768
HID = 1024
NODE_DEV = 512
TILE = 128
SLOTS = 6
CAP = 32
HUB_DEV = 4
REACH = 4
NODES = 16384
HUBS = 128
HALO = 256
COLS = 896
CBLK = 7
RBLK = 4
N_DOM = 32


def draw_send_counts(key, part):
    key = jax.random.fold_in(key, 11)
    source = jnp.arange(N_DOM, dtype=jnp.int32)[:, None]
    target = jnp.arange(N_DOM, dtype=jnp.int32)[None, :]
    offset = (target - source) % N_DOM
    nearby = (offset >= 1) & (offset <= REACH) | (offset >= N_DOM - REACH)
    lowest = max(1, (CAP + 2) // 3)
    counts = jax.random.randint(key, (N_DOM, N_DOM), lowest, CAP + 1)
    counts = jnp.where(offset == 1, CAP, counts)
    return jnp.where(nearby, counts, 0).astype(jnp.int32)


def with_ends(entries, key, smallest, largest):
    index_at = [jax.random.randint(jax.random.fold_in(key, axis), (), 0, length) for axis, length in enumerate(entries.shape)]
    longest = entries.shape.index(max(entries.shape))
    next_to = index_at[:longest] + [(index_at[longest] + 1) % entries.shape[longest]] + index_at[longest + 1:]
    return entries.at[tuple(index_at)].set(smallest).at[tuple(next_to)].set(largest)


def block_levels(stream_key, shape, split, least, largest):
    loudness, own = 1.0, jax.random.fold_in(stream_key, 6)
    for axis_at, shards_of in split:
        heights = jnp.exp(jax.random.uniform(jax.random.fold_in(own, axis_at), (shards_of,), jnp.float32, least / len(split), largest / len(split)))
        loudness = loudness * jnp.repeat(heights, shape[axis_at] // shards_of).reshape([-1 if axis == axis_at else 1 for axis in range(len(shape))])
    return loudness


def centred(stream_key, dims, deviation, bound, pieces=(), kind=jnp.bfloat16):
    loudness = block_levels(stream_key, dims, pieces, -0.22, 0.18) if pieces else 1.0
    array = jax.random.normal(stream_key, dims, jnp.float32) * deviation * loudness
    return jnp.minimum(jnp.maximum(array, -bound), bound).astype(kind)


def setup_inputs(seed: int = 0) -> dict:
    splits = jax.random.split(jax.random.key(seed), 11)
    features = centred(splits[0], (NODES, F), 1.0, 6.0, ((0, 32),))
    w_self = centred(splits[1], (F, HID), F ** -0.5, 0.21875)
    w_neigh = centred(splits[2], (F, HID), F ** -0.5, 0.21875)
    tile_cols = with_ends(jax.random.randint(splits[3], (NODES // TILE, SLOTS), 0, CBLK), jax.random.fold_in(splits[3], 1), 0, CBLK - 1).astype(jnp.int32)
    tile_weights = with_ends(jax.random.randint(splits[4], (NODES // TILE, SLOTS, TILE, TILE), 0, 4), jax.random.fold_in(splits[4], 1), 0, 3).astype(jnp.int32)
    send_rows = with_ends(jax.random.randint(splits[5], (N_DOM, N_DOM, CAP), 0, NODE_DEV), jax.random.fold_in(splits[5], 1), 0, NODE_DEV - 1).astype(jnp.int32)
    send_counts = draw_send_counts(jax.random.fold_in(splits[10], 71), 0)
    hub_rows = with_ends(jax.random.randint(splits[7], (N_DOM, HUB_DEV), 0, NODE_DEV), jax.random.fold_in(splits[7], 1), 0, NODE_DEV - 1).astype(jnp.int32)
    readers = with_ends((jax.random.randint(splits[8], (N_DOM, HUBS), 0, 2) < 1).astype(jnp.int32), jax.random.fold_in(splits[8], 1), 0, 1)
    cotangent = centred(splits[9], (NODES, HID), 1.0, 6.0, ((0, 32),))
    return dict(features=features, w_self=w_self, w_neigh=w_neigh, tile_cols=tile_cols, tile_weights=tile_weights, send_rows=send_rows, send_counts=send_counts, hub_rows=hub_rows, readers=readers, cotangent=cotangent)


def reference(features, w_self, w_neigh, tile_cols, tile_weights, send_rows, send_counts, hub_rows, readers, cotangent):
    rows = NODE_DEV
    width = features.shape[1]
    highest = lax.Precision.HIGHEST
    owners = jnp.arange(N_DOM, dtype=jnp.int32)
    hub_index = (owners[:, None] * rows + hub_rows).reshape(-1).astype(jnp.int32)
    hub_all = features[hub_index]
    slot_ids = jnp.arange(CAP, dtype=jnp.int32)
    step_ids = jnp.arange(2 * REACH, dtype=jnp.int32)
    distance = jnp.where(step_ids < REACH, step_ids + 1, REACH - 1 - step_ids).astype(jnp.int32)
    weights_all = tile_weights.astype(jnp.float32).reshape(N_DOM, RBLK, SLOTS, TILE, TILE)
    cols_all = tile_cols.reshape(N_DOM, RBLK, SLOTS)
    inverse_all = 1.0 / (jnp.sum(weights_all, axis=(2, 4)) + 1.0)

    def halo_lists(device):
        sources = ((device - distance) % N_DOM).astype(jnp.int32)
        lists = send_rows[sources, device]
        index = (sources[:, None] * rows + lists).astype(jnp.int32)
        live = slot_ids[None, :] < send_counts[sources, device][:, None]
        return index.reshape(-1), live.reshape(-1)

    def aggregate(device):
        local = lax.dynamic_slice_in_dim(features, device * rows, rows, 0)
        index, live = halo_lists(device)
        halo = features[index] * live[:, None].astype(jnp.bfloat16)
        flag = readers[device].astype(jnp.bfloat16)
        stacked = jnp.concatenate([local, halo, hub_all * flag[:, None]], axis=0)
        blocks = stacked.astype(jnp.float32).reshape(CBLK, TILE, width)
        picked = blocks[cols_all[device]]
        total = jnp.einsum("rkij,rkjf->rif", weights_all[device], picked, precision=highest)
        return (total * inverse_all[device][:, :, None]).reshape(rows, width).astype(jnp.bfloat16)

    neigh = lax.map(aggregate, owners).reshape(NODES, width)
    pre = jnp.dot(features, w_self, preferred_element_type=jnp.float32) + jnp.dot(neigh, w_neigh, preferred_element_type=jnp.float32)
    out_rows = jax.nn.silu(pre).astype(jnp.bfloat16)
    sigma = jax.nn.sigmoid(pre)
    dpre = (cotangent.astype(jnp.float32) * sigma * (1.0 + pre * (1.0 - sigma))).astype(jnp.bfloat16)
    grad_self = jnp.dot(features.T, dpre, preferred_element_type=jnp.float32)
    grad_neigh = jnp.dot(neigh.T, dpre, preferred_element_type=jnp.float32)
    dself = jnp.dot(dpre, w_self.T, preferred_element_type=jnp.float32)
    dmiddle = jnp.dot(dpre, w_neigh.T, preferred_element_type=jnp.float32)
    dneigh = (dmiddle.reshape(N_DOM, RBLK, TILE, width) * inverse_all[:, :, :, None]).astype(jnp.bfloat16)

    def spread(carry, device):
        grad, hub_total = carry
        scaled = dneigh[device].astype(jnp.float32)
        contrib = jnp.einsum("rkij,rif->rkjf", weights_all[device], scaled, precision=highest)
        dstack = jnp.zeros((CBLK, TILE, width), jnp.float32).at[cols_all[device].reshape(-1)].add(contrib.reshape(-1, TILE, width)).reshape(COLS, width)
        current = lax.dynamic_slice_in_dim(grad, device * rows, rows, 0)
        grad = lax.dynamic_update_slice_in_dim(grad, current + dstack[:rows], device * rows, 0)
        index, live = halo_lists(device)
        halo_part = dstack[rows:rows + HALO] * live[:, None].astype(jnp.float32)
        grad = grad.at[index].add(halo_part)
        hub_total = hub_total + dstack[rows + HALO:] * readers[device].astype(jnp.float32)[:, None]
        return (grad, hub_total), None

    start = (dself, jnp.zeros((HUBS, width), jnp.float32))
    (grad, hub_total), unused = lax.scan(spread, start, owners)
    grad = grad.at[hub_index].add(hub_total)
    return out_rows, grad.astype(jnp.bfloat16), grad_self, grad_neigh
```

```python
import functools

import jax
import jax.numpy as jnp
from jax import lax
from jax.experimental import pallas as pl
from jax.experimental.pallas import tpu as pltpu
from jax.sharding import PartitionSpec as P

REACH = 4
MESH = pl.DeviceIdType.MESH
F32 = jnp.float32
BF16 = jnp.bfloat16
GROUPS = 3


def near_offsets(reach):
    return list(range(1, reach + 1)) + [-distance for distance in range(1, reach + 1)]


def bit_orders(peers):
    bits = list(range(1, peers.bit_length() - 1))
    head, tail = bits[:-1], bits[-1:]
    orders = []
    for group in range(GROUPS):
        turn = group * len(head) // GROUPS
        orders.append(head[turn:] + head[:turn] + tail)
    return orders


def halves(rows, cols, steps):
    sizes = [(rows, cols)]
    for _ in range(steps):
        rows, cols = (rows // 2, cols) if rows > 16 else (rows, cols // 2)
        sizes.append((rows, cols))
    return sizes


def dot(left, right, dims=((1,), (0,))):
    return lax.dot_general(left, right, (dims, ((), ())), preferred_element_type=F32)


def layer(peers, offsets, sizes, cols_ref, feat_ref, ws_ref, wn_ref, tiles_ref, pick_ref, flag_ref, cot_ref,
          out_ref, gfeat_ref, res_ref, *scratch):
    steps = len(sizes) - 1
    (x, adj, inv, scat, going, halo, hub_out, hub_in, hub_all, pre, dpre, dneigh, own, back_out, back,
     hback_out, hback, core_out, core_in, acc) = scratch[:20]
    rs_out, rs_in = scratch[20:20 + steps], scratch[20 + steps:20 + 2 * steps]
    (halo_s, halo_r, hub_s, hub_r, back_s, back_r, hback_s, hback_r, core_s, core_r, rs_s, rs_r,
     ag_s, ag_r, last_s, last_r) = scratch[20 + 2 * steps:]
    me = lax.axis_index("dom")
    core = me % 2
    mate = me + 1 - 2 * core
    rows, width = feat_ref.shape
    hid = ws_ref.shape[1]
    row_blocks, slots, tile, _ = tiles_ref.shape
    col_blocks = adj.shape[1] // tile
    caps = halo.shape[0]
    orders = bit_orders(peers)
    grows = width // GROUPS

    def remote(src, dst, send, recv, peer):
        return pltpu.make_async_remote_copy(
            src_ref=src, dst_ref=dst, send_sem=send, recv_sem=recv, device_id=(peer,), device_id_type=MESH
        )

    barrier = pltpu.get_barrier_semaphore()

    def greet(k, carry):
        pl.semaphore_signal(barrier, inc=1, device_id=(lax.rem(me + k, peers),), device_id_type=MESH)
        return carry

    lax.fori_loop(1, peers, greet, 0)

    picks = pick_ref.shape[1]
    scat[...] = (lax.broadcasted_iota(jnp.int32, (rows, picks), 0) == pick_ref[...]).astype(F32).astype(BF16)
    x[0] = feat_ref[...]
    picked = dot(scat[...], feat_ref[...], ((0,), (0,)))
    going[...] = picked[:caps].astype(BF16)
    hub_out[...] = picked[caps:caps + 4]
    hub_in[me] = picked[caps:caps + 4]
    pl.semaphore_wait(barrier, peers - 1)

    part = caps // len(offsets)

    def halo_copy(q):
        piece = pl.ds(q * part, part)
        return remote(going.at[piece], halo.at[piece], halo_s.at[q], halo_r.at[q],
                      lax.rem(me + offsets[q] + peers, peers))

    def hub_copy(k):
        return remote(hub_out, hub_in.at[me], hub_s.at[k], hub_r.at[k], lax.rem(me + k, peers))

    def back_copy(q):
        piece = pl.ds(q * part, part)
        return remote(back_out.at[piece], back.at[piece], back_s.at[q], back_r.at[q],
                      lax.rem(me - offsets[q] + peers, peers))

    def hback_copy(k):
        peer = lax.rem(me + k, peers)
        return remote(hback_out.at[peer], hback.at[me], hback_s.at[k], hback_r.at[k], peer)

    def start_all(make):
        def body(k, carry):
            make(k).start()
            return carry
        lax.fori_loop(1, peers, body, 0)

    def wait_recv_all(make):
        def body(k, carry):
            make(k).wait_recv()
            return carry
        lax.fori_loop(1, peers, body, 0)

    def wait_send_all(make):
        def body(k, carry):
            make(k).wait_send()
            return carry
        lax.fori_loop(1, peers, body, 0)

    start_all(hub_copy)
    for q in range(len(offsets)):
        halo_copy(q).start()

    def build(b, carry):
        weights = [tiles_ref[b, k].astype(F32) for k in range(slots)]
        at = pl.ds(pl.multiple_of(b * tile, tile), tile)
        inv[at, :] = 1.0 / (jnp.sum(sum(weights), axis=1, keepdims=True) + 1.0)
        for t in range(col_blocks):
            total = jnp.zeros((tile, tile), F32)
            for k in range(slots):
                total = total + weights[k] * (cols_ref[b, k] == t).astype(F32)
            if t * tile >= rows + caps:
                first = t * tile - rows - caps
                total = total * flag_ref[:, first:first + tile].astype(F32)
            adj[at, t * tile:(t + 1) * tile] = total.astype(BF16)
        return carry

    lax.fori_loop(0, row_blocks, build, 0)
    half = rows // 2
    for r in range(2):
        at = slice(r * half, (r + 1) * half)
        own[at] = dot(adj[at, :rows], feat_ref[...])
        pre[at] = dot(feat_ref[at], ws_ref[...])

    for q in range(len(offsets)):
        halo_copy(q).wait_recv()
    wait_recv_all(hub_copy)
    for j in range(0, peers, 4):
        hub_all[4 * j:4 * j + 16] = jnp.concatenate([hub_in[j + i] for i in range(4)], axis=0).astype(BF16)

    for r in range(2):
        at = slice(r * half, (r + 1) * half)
        total = own[at] + dot(adj[at, rows:rows + caps], halo[...]) + dot(adj[at, rows + caps:], hub_all[...])
        neigh = (total * inv[at]).astype(BF16)
        x[1, at] = neigh
        whole = pre[at] + dot(neigh, wn_ref[...])
        sigma = jax.nn.sigmoid(whole)
        out_ref[at] = (whole * sigma).astype(BF16)
        dpre[at] = (cot_ref[at].astype(F32) * sigma * (1.0 + whole * (1.0 - sigma))).astype(BF16)

    def core_copy(g):
        return remote(core_out.at[g], core_in.at[g], core_s.at[g], core_r.at[g], mate)

    for g in range(GROUPS):
        core_out[g] = dot(x[1 - core, :, g * grows:(g + 1) * grows], dpre[...], ((0,), (0,))).astype(BF16)
        core_copy(g).start()
    for g in range(GROUPS):
        acc[g] = dot(x[core, :, g * grows:(g + 1) * grows], dpre[...], ((0,), (0,)))

    zero = me * 0
    places = [(zero, zero)] * GROUPS
    trail = [[None] * steps for _ in range(GROUPS)]

    def ds(row, col, size):
        unit = min(size[0], grows)
        return (pl.ds(pl.multiple_of(row, 16), unit), pl.ds(pl.multiple_of(col, 128), size[1]))

    def rs_copy(s, g):
        step = 2 ** orders[g][s]
        bit = (me // step) % 2
        return remote(rs_out[s].at[g], rs_in[s].at[g], rs_s.at[s, g], rs_r.at[s, g], me + step - 2 * step * bit)

    def rs_start(s, g):
        row, col = places[g]
        size = sizes[s + 1]
        bit = (me // 2 ** orders[g][s]) % 2
        if size[0] != sizes[s][0]:
            keep, give = (row + bit * size[0], col), (row + (1 - bit) * size[0], col)
        else:
            keep, give = (row, col + bit * size[1]), (row, col + (1 - bit) * size[1])
        rs_out[s][g] = acc[(g, *ds(*give, size))].astype(BF16)
        rs_copy(s, g).start()
        places[g] = keep

    def rs_end(s, g):
        rs_copy(s, g).wait_recv()
        spot = (g, *ds(*places[g], sizes[s + 1]))
        acc[spot] = acc[spot] + rs_in[s][g].astype(F32)

    def ag_place(s, g):
        row, col = zero, zero
        for t in range(s + 1):
            bit = (me // 2 ** orders[g][t]) % 2
            if sizes[t + 1][0] != sizes[t][0]:
                row = row + bit * sizes[t + 1][0]
            else:
                col = col + bit * sizes[t + 1][1]
        return row, col

    def ag_copy(s, g):
        step = 2 ** orders[g][s]
        bit = (me // step) % 2
        row, col = ag_place(s, g)
        size = sizes[s + 1]
        spot = res_ref.at[(core, *ds(row + g * grows, col, size))]
        return remote(spot, spot, ag_s.at[s, g], ag_r.at[s, g], me + step - 2 * step * bit)

    def last_copy(g):
        spot = res_ref.at[core, pl.ds(g * grows, grows)]
        return remote(spot, spot, last_s.at[g], last_r.at[g], mate)

    for g in range(GROUPS):
        core_copy(g).wait_recv()
        acc[g] = acc[g] + core_in[g].astype(F32)
        rs_start(0, g)

    for r in range(2):
        at = slice(r * half, (r + 1) * half)
        dneigh[at] = (dot(dpre[at], wn_ref[...], ((1,), (1,))) * inv[at]).astype(BF16)
    back_out[...] = dot(adj[:, rows:rows + caps], dneigh[...], ((0,), (0,))).astype(BF16)
    hubs = dot(adj[:, rows + caps:], dneigh[...], ((0,), (0,)))
    for j in range(peers):
        hback_out[j] = hubs[4 * j:4 * j + 4]
    hback[me] = hback_out[me]
    for q in range(len(offsets)):
        back_copy(q).start()
    start_all(hback_copy)

    for s in range(steps):
        for g in range(GROUPS):
            rs_end(s, g)
            if s + 1 < steps:
                rs_start(s + 1, g)
            else:
                spot = ds(places[g][0] + g * grows, places[g][1], sizes[steps])
                res_ref[(core, *spot)] = acc[(g, *ds(*places[g], sizes[steps]))].astype(BF16)
                ag_copy(steps - 1, g).start()
        if s == 0:
            for r in range(2):
                at = slice(r * half, (r + 1) * half)
                own[at] = dot(dpre[at], ws_ref[...], ((1,), (1,)))
            own[...] += dot(adj[:, :rows], dneigh[...], ((0,), (0,)))

    for s in reversed(range(steps)):
        for g in range(GROUPS):
            ag_copy(s, g).wait_recv()
            if s > 0:
                ag_copy(s - 1, g).start()
            else:
                last_copy(g).start()

    for q in range(len(offsets)):
        back_copy(q).wait_recv()
    wait_recv_all(hback_copy)
    hub_sum = jnp.sum(hback[...], axis=0)
    coarse = hub_sum.astype(BF16).astype(F32)
    hub_part = jnp.concatenate(
        [coarse, hub_sum - coarse, jnp.zeros((picks - caps - 8, width), F32)], axis=0
    ).astype(BF16)
    for r in range(2):
        at = slice(r * half, (r + 1) * half)
        total = own[at] + dot(scat[at, :caps], back[...]) + dot(scat[at, caps:], hub_part)
        gfeat_ref[at] = total.astype(BF16)

    for g in range(GROUPS):
        last_copy(g).wait_recv()
    for q in range(len(offsets)):
        halo_copy(q).wait_send()
        back_copy(q).wait_send()
    wait_send_all(hub_copy)
    wait_send_all(hback_copy)
    for g in range(GROUPS):
        core_copy(g).wait_send()
        last_copy(g).wait_send()
        for s in range(steps):
            rs_copy(s, g).wait_send()
            ag_copy(s, g).wait_send()


def on_device(peers, features, w_self, w_neigh, tile_cols, tile_weights, send_rows, send_counts, hub_rows, readers,
              cotangent):
    me = lax.axis_index("dom")
    rows, width = features.shape
    hid = w_self.shape[1]
    cap = send_rows.shape[2]
    offsets = near_offsets(REACH)
    caps = len(offsets) * cap
    hubs = readers.shape[1]
    tile = tile_weights.shape[2]
    targets = jnp.where(
        jnp.arange(cap, dtype=jnp.int32)[None, :] < send_counts[0][:, None], send_rows[0], -1
    )
    wrapped = jnp.concatenate([targets[-REACH:], targets, targets[:REACH]], axis=0)
    window = lax.dynamic_slice_in_dim(wrapped, me, 2 * REACH + 1, 0)
    lists = [window[REACH + offset] for offset in offsets]
    spare = jnp.full((tile - 2 * hub_rows.shape[1],), -1, jnp.int32)
    pick = jnp.concatenate(lists + [hub_rows[0], hub_rows[0], spare])[None, :]
    picks = pick.shape[1]

    steps = peers.bit_length() - 2
    grows = width // GROUPS
    sizes = halves(grows, hid, steps)
    dma = pltpu.SemaphoreType.DMA
    vmem = pltpu.VMEM
    scratch = [
        vmem((2, rows, width), BF16),
        vmem((rows, rows + caps + hubs), BF16),
        vmem((rows, 1), F32),
        vmem((rows, picks), BF16),
        vmem((caps, width), BF16),
        vmem((caps, width), BF16),
        vmem((4, width), F32),
        vmem((peers, 4, width), F32),
        vmem((hubs, width), BF16),
        vmem((rows, hid), F32),
        vmem((rows, hid), BF16),
        vmem((rows, width), BF16),
        vmem((rows, width), F32),
        vmem((caps, width), BF16),
        vmem((caps, width), BF16),
        vmem((peers, 4, width), F32),
        vmem((peers, 4, width), F32),
        vmem((GROUPS, grows, hid), BF16),
        vmem((GROUPS, grows, hid), BF16),
        vmem((GROUPS, grows, hid), F32),
    ]
    scratch += [vmem((GROUPS, *sizes[s + 1]), BF16) for s in range(steps)] * 2
    q = len(offsets)
    scratch += [
        dma((q,)), dma((q,)), dma((peers,)), dma((peers,)), dma((q,)), dma((q,)), dma((peers,)), dma((peers,)),
        dma((GROUPS,)), dma((GROUPS,)), dma((steps, GROUPS)), dma((steps, GROUPS)),
        dma((steps, GROUPS)), dma((steps, GROUPS)), dma((GROUPS,)), dma((GROUPS,)),
    ]
    whole = pl.BlockSpec(memory_space=pltpu.VMEM)
    out_rows, grad, both = pl.pallas_call(
        functools.partial(layer, peers, offsets, sizes),
        out_shape=(
            jax.ShapeDtypeStruct((rows, hid), BF16),
            jax.ShapeDtypeStruct((rows, width), BF16),
            jax.ShapeDtypeStruct((2, width, hid), BF16),
        ),
        in_specs=[pl.BlockSpec(memory_space=pltpu.SMEM)] + [whole] * 7,
        out_specs=(whole,) * 3,
        scratch_shapes=scratch,
        compiler_params=pltpu.CompilerParams(
            collective_id=0, has_side_effects=True, vmem_limit_bytes=56 * 1024 * 1024
        ),
        cost_estimate=pl.CostEstimate(
            flops=8 * 2 * rows * width * hid, bytes_accessed=16 * rows * width * 2, transcendentals=rows * hid
        ),
    )(tile_cols, features, w_self, w_neigh, tile_weights, pick, readers, cotangent)
    return out_rows, grad, both[0].astype(F32), both[1].astype(F32)


def solution(mesh):
    peers = mesh.shape["dom"]
    return jax.shard_map(
        functools.partial(on_device, peers),
        mesh=mesh,
        in_specs=(
            P("dom", None),
            P(),
            P(),
            P("dom", None),
            P("dom", None, None, None),
            P("dom", None, None),
            P("dom", None),
            P("dom", None),
            P("dom", None),
            P("dom", None),
        ),
        out_specs=(P("dom", None), P("dom", None), P(), P()),
        check_vma=False,
    )
```

```python
import functools

import jax
import jax.numpy as jnp
from jax import lax
from jax.experimental import pallas as pl
from jax.experimental.pallas import tpu as pltpu
from jax.sharding import PartitionSpec as P

REACH = 4
MESH = pl.DeviceIdType.MESH
F32 = jnp.float32
BF16 = jnp.bfloat16
GROUPS = 6
QUAD = 4


def near_offsets(reach):
    return list(range(1, reach + 1)) + [-distance for distance in range(1, reach + 1)]


def bit_orders(peers):
    bits = list(range(1, peers.bit_length() - 1))
    head, tail = bits[:-1], bits[-1:]
    orders = []
    for group in range(GROUPS):
        turn = (group % 3) * len(head) // 3
        order = head[turn:] + head[:turn]
        if group >= 3:
            order = order[:1] + order[:0:-1]
        orders.append(order + tail)
    return orders


def halves(rows, cols, steps):
    sizes = [(rows, cols)]
    for _ in range(steps):
        rows, cols = (rows // 2, cols) if rows > 16 else (rows, cols // 2)
        sizes.append((rows, cols))
    return sizes


def dot(left, right, dims=((1,), (0,))):
    return lax.dot_general(left, right, (dims, ((), ())), preferred_element_type=F32)


def layer(peers, offsets, sizes, cols_ref, feat_hbm, ws_hbm, wn_hbm, tiles_hbm, pick_ref, flag_ref, cot_hbm,
          out_ref, gfeat_ref, res_ref, *scratch):
    steps = len(sizes) - 1
    (x, adj, inv, scat, going, halo, hub_out, hub_in, hub_all, pre, dpre, dneigh, own, back_out, back,
     hback_out, hback, core_out, core_in, acc, ws_ref, wn_ref, tiles_ref, cot_ref, fold_out, fold_in) = scratch[:26]
    rs_out, rs_in = scratch[26:26 + steps], scratch[26 + steps:26 + 2 * steps]
    (halo_s, halo_r, hub_s, hub_r, back_s, back_r, hback_s, hback_r, core_s, core_r, rs_s, rs_r,
     ag_s, ag_r, last_s, last_r, load_s, quad_s, quad_r, fold_s, fold_r) = scratch[26 + 2 * steps:]
    feat_ref = x.at[0]
    loads = [
        pltpu.make_async_copy(source, target, load_s.at[i])
        for i, (source, target) in enumerate(
            [(feat_hbm, feat_ref), (tiles_hbm, tiles_ref), (ws_hbm, ws_ref), (wn_hbm, wn_ref), (cot_hbm, cot_ref)]
        )
    ]
    for load in loads:
        load.start()
    seat = lax.axis_index("dom") % QUAD
    far = peers // QUAD
    me = lax.axis_index("dom")
    core = me % 2
    mate = me + 1 - 2 * core
    rows, width = x.shape[1:]
    hid = ws_ref.shape[1]
    row_blocks, slots, tile, _ = tiles_ref.shape
    col_blocks = adj.shape[1] // tile
    caps = halo.shape[0]
    orders = bit_orders(peers)
    grows = width // GROUPS

    def remote(src, dst, send, recv, peer):
        return pltpu.make_async_remote_copy(
            src_ref=src, dst_ref=dst, send_sem=send, recv_sem=recv, device_id=(peer,), device_id_type=MESH
        )

    barrier = pltpu.get_barrier_semaphore()

    def greet(k, carry):
        pl.semaphore_signal(barrier, inc=1, device_id=(lax.rem(me + k, peers),), device_id_type=MESH)
        return carry

    lax.fori_loop(1, peers, greet, 0)

    picks = pick_ref.shape[1]
    scat[...] = (lax.broadcasted_iota(jnp.int32, (rows, picks), 0) == pick_ref[...]).astype(F32).astype(BF16)
    loads[0].wait()
    picked = dot(scat[...], feat_ref[...], ((0,), (0,)))
    going[...] = picked[:caps].astype(BF16)
    hub_out[...] = picked[caps:caps + 4]
    hub_in[me // QUAD] = picked[caps:caps + 4]
    pl.semaphore_wait(barrier, peers - 1)

    part = caps // len(offsets)

    def halo_copy(q):
        piece = pl.ds(q * part, part)
        return remote(going.at[piece], halo.at[piece], halo_s.at[q], halo_r.at[q],
                      lax.rem(me + offsets[q] + peers, peers))

    def hub_copy(k):
        return remote(hub_out, hub_in.at[me // QUAD], hub_s.at[k], hub_r.at[k], lax.rem(me + QUAD * k, peers))

    def mate_of(k):
        return me - seat + (seat + k) % QUAD

    def quad_copy(k):
        return remote(hub_all.at[seat], hub_all.at[seat], quad_s.at[k], quad_r.at[k], mate_of(k))

    def fold_copy(k):
        return remote(fold_out.at[(seat + k) % QUAD], fold_in.at[seat], fold_s.at[k], fold_r.at[k], mate_of(k))

    def back_copy(q):
        piece = pl.ds(q * part, part)
        return remote(back_out.at[piece], back.at[piece], back_s.at[q], back_r.at[q],
                      lax.rem(me - offsets[q] + peers, peers))

    def hback_copy(k):
        peer = lax.rem(me + QUAD * k, peers)
        return remote(hback_out.at[peer // QUAD], hback.at[me // QUAD], hback_s.at[k], hback_r.at[k], peer)

    def start_all(make):
        def body(k, carry):
            make(k).start()
            return carry
        lax.fori_loop(1, far, body, 0)

    def wait_recv_all(make):
        def body(k, carry):
            make(k).wait_recv()
            return carry
        lax.fori_loop(1, far, body, 0)

    def wait_send_all(make):
        def body(k, carry):
            make(k).wait_send()
            return carry
        lax.fori_loop(1, far, body, 0)

    start_all(hub_copy)
    for q in range(len(offsets)):
        halo_copy(q).start()

    def build(b, carry):
        weights = [tiles_ref[b, k].astype(F32) for k in range(slots)]
        at = pl.ds(pl.multiple_of(b * tile, tile), tile)
        inv[at, :] = 1.0 / (jnp.sum(sum(weights), axis=1, keepdims=True) + 1.0)
        for t in range(col_blocks):
            total = jnp.zeros((tile, tile), F32)
            for k in range(slots):
                total = total + weights[k] * (cols_ref[b, k] == t).astype(F32)
            if t * tile >= rows + caps:
                first = t * tile - rows - caps
                total = total * flag_ref[:, first:first + tile].astype(F32)
            adj[at, t * tile:(t + 1) * tile] = total.astype(BF16)
        return carry

    loads[1].wait()
    lax.fori_loop(0, row_blocks, build, 0)
    hubs = peers * 4
    made = lax.broadcasted_iota(jnp.int32, (hubs, hubs), 0)
    wanted = (made // 4) % QUAD * peers + made // (4 * QUAD) * 4 + made % 4
    turned = (lax.broadcasted_iota(jnp.int32, (hubs, hubs), 1) == wanted).astype(F32).astype(BF16)
    adj[:, rows + caps:] = dot(adj[:, rows + caps:], turned).astype(BF16)
    wait_recv_all(hub_copy)
    hub_all[seat] = jnp.concatenate([hub_in[j] for j in range(far)], axis=0).astype(BF16)
    for k in range(1, QUAD):
        quad_copy(k).start()
    loads[2].wait()
    half = rows // 2
    for r in range(2):
        at = slice(r * half, (r + 1) * half)
        own[at] = dot(adj[at, :rows], feat_ref[...])
        pre[at] = dot(feat_ref[at], ws_ref[...])

    for q in range(len(offsets)):
        halo_copy(q).wait_recv()
    for k in range(1, QUAD):
        quad_copy(k).wait_recv()
    loads[3].wait()
    loads[4].wait()

    for r in range(2):
        at = slice(r * half, (r + 1) * half)
        total = own[at] + dot(adj[at, rows:rows + caps], halo[...]) + dot(adj[at, rows + caps:], hub_all[...].reshape(hubs, width))
        neigh = (total * inv[at]).astype(BF16)
        x[1, at] = neigh
        whole = pre[at] + dot(neigh, wn_ref[...])
        sigma = jax.nn.sigmoid(whole)
        out_ref[at] = (whole * sigma).astype(BF16)
        dpre[at] = (cot_ref[at].astype(F32) * sigma * (1.0 + whole * (1.0 - sigma))).astype(BF16)

    def core_copy(g):
        return remote(core_out.at[g], core_in.at[g], core_s.at[g], core_r.at[g], mate)

    for g in range(0, GROUPS, 2):
        term = dot(x[1 - core, :, g * grows:(g + 2) * grows], dpre[...], ((0,), (0,))).astype(BF16)
        for i in range(2):
            core_out[g + i] = term[i * grows:(i + 1) * grows]
            core_copy(g + i).start()
    for g in range(0, GROUPS, 2):
        term = dot(x[core, :, g * grows:(g + 2) * grows], dpre[...], ((0,), (0,)))
        for i in range(2):
            acc[g + i] = term[i * grows:(i + 1) * grows]

    zero = me * 0
    places = [(zero, zero)] * GROUPS
    trail = [[None] * steps for _ in range(GROUPS)]

    def ds(row, col, size):
        unit = min(size[0], grows)
        return (pl.ds(pl.multiple_of(row, 16), unit), pl.ds(pl.multiple_of(col, 128), size[1]))

    def rs_copy(s, g):
        step = 2 ** orders[g][s]
        bit = (me // step) % 2
        return remote(rs_out[s].at[g], rs_in[s].at[g], rs_s.at[s, g], rs_r.at[s, g], me + step - 2 * step * bit)

    def rs_start(s, g):
        row, col = places[g]
        size = sizes[s + 1]
        bit = (me // 2 ** orders[g][s]) % 2
        if size[0] != sizes[s][0]:
            keep, give = (row + bit * size[0], col), (row + (1 - bit) * size[0], col)
        else:
            keep, give = (row, col + bit * size[1]), (row, col + (1 - bit) * size[1])
        rs_out[s][g] = acc[(g, *ds(*give, size))].astype(BF16)
        rs_copy(s, g).start()
        places[g] = keep

    def rs_end(s, g):
        rs_copy(s, g).wait_recv()
        spot = (g, *ds(*places[g], sizes[s + 1]))
        acc[spot] = acc[spot] + rs_in[s][g].astype(F32)

    def ag_place(s, g):
        row, col = zero, zero
        for t in range(s + 1):
            bit = (me // 2 ** orders[g][t]) % 2
            if sizes[t + 1][0] != sizes[t][0]:
                row = row + bit * sizes[t + 1][0]
            else:
                col = col + bit * sizes[t + 1][1]
        return row, col

    def ag_copy(s, g):
        step = 2 ** orders[g][s]
        bit = (me // step) % 2
        row, col = ag_place(s, g)
        size = sizes[s + 1]
        spot = res_ref.at[(core, *ds(row + g * grows, col, size))]
        return remote(spot, spot, ag_s.at[s, g], ag_r.at[s, g], me + step - 2 * step * bit)

    def last_copy(g):
        spot = res_ref.at[core, pl.ds(g * grows, grows)]
        return remote(spot, spot, last_s.at[g], last_r.at[g], mate)

    for g in range(GROUPS):
        core_copy(g).wait_recv()
        acc[g] = acc[g] + core_in[g].astype(F32)
        rs_start(0, g)

    for r in range(2):
        at = slice(r * half, (r + 1) * half)
        dneigh[at] = (dot(dpre[at], wn_ref[...], ((1,), (1,))) * inv[at]).astype(BF16)
    back_out[...] = dot(adj[:, rows:rows + caps], dneigh[...], ((0,), (0,))).astype(BF16)
    for q in range(len(offsets)):
        back_copy(q).start()
    fold_out[...] = dot(adj[:, rows + caps:], dneigh[...], ((0,), (0,))).astype(BF16).reshape(QUAD, peers, width)
    fold_in[seat] = fold_out[seat]
    for k in range(1, QUAD):
        fold_copy(k).start()

    for s in range(steps):
        for g in range(GROUPS):
            rs_end(s, g)
            if s + 1 < steps:
                rs_start(s + 1, g)
            else:
                spot = ds(places[g][0] + g * grows, places[g][1], sizes[steps])
                res_ref[(core, *spot)] = acc[(g, *ds(*places[g], sizes[steps]))].astype(BF16)
                ag_copy(steps - 1, g).start()
        if s == 0:
            for r in range(2):
                at = slice(r * half, (r + 1) * half)
                own[at] = dot(dpre[at], ws_ref[...], ((1,), (1,)))
        elif s == 1:
            own[...] += dot(adj[:, :rows], dneigh[...], ((0,), (0,)))
            for k in range(1, QUAD):
                fold_copy(k).wait_recv()
            fold = jnp.sum(fold_in[...].astype(F32), axis=0)
            for j in range(far):
                hback_out[j] = fold[4 * j:4 * j + 4]
            hback[me // QUAD] = hback_out[me // QUAD]
            start_all(hback_copy)

    for s in reversed(range(steps)):
        for g in range(GROUPS):
            ag_copy(s, g).wait_recv()
            if s > 0:
                ag_copy(s - 1, g).start()
            else:
                last_copy(g).start()

    for q in range(len(offsets)):
        back_copy(q).wait_recv()
    wait_recv_all(hback_copy)
    hub_sum = jnp.sum(hback[...], axis=0)
    coarse = hub_sum.astype(BF16).astype(F32)
    hub_part = jnp.concatenate(
        [coarse, hub_sum - coarse, jnp.zeros((picks - caps - 8, width), F32)], axis=0
    ).astype(BF16)
    for r in range(2):
        at = slice(r * half, (r + 1) * half)
        total = own[at] + dot(scat[at, :caps], back[...]) + dot(scat[at, caps:], hub_part)
        gfeat_ref[at] = total.astype(BF16)

    for g in range(GROUPS):
        last_copy(g).wait_recv()
    for q in range(len(offsets)):
        halo_copy(q).wait_send()
        back_copy(q).wait_send()
    for k in range(1, QUAD):
        quad_copy(k).wait_send()
        fold_copy(k).wait_send()
    wait_send_all(hub_copy)
    wait_send_all(hback_copy)
    for g in range(GROUPS):
        core_copy(g).wait_send()
        last_copy(g).wait_send()
        for s in range(steps):
            rs_copy(s, g).wait_send()
            ag_copy(s, g).wait_send()


def on_device(peers, features, w_self, w_neigh, tile_cols, tile_weights, send_rows, send_counts, hub_rows, readers,
              cotangent):
    me = lax.axis_index("dom")
    rows, width = features.shape
    hid = w_self.shape[1]
    cap = send_rows.shape[2]
    offsets = near_offsets(REACH)
    caps = len(offsets) * cap
    hubs = readers.shape[1]
    tile = tile_weights.shape[2]
    targets = jnp.where(
        jnp.arange(cap, dtype=jnp.int32)[None, :] < send_counts[0][:, None], send_rows[0], -1
    )
    wrapped = jnp.concatenate([targets[-REACH:], targets, targets[:REACH]], axis=0)
    window = lax.dynamic_slice_in_dim(wrapped, me, 2 * REACH + 1, 0)
    lists = [window[REACH + offset] for offset in offsets]
    spare = jnp.full((tile - 2 * hub_rows.shape[1],), -1, jnp.int32)
    pick = jnp.concatenate(lists + [hub_rows[0], hub_rows[0], spare])[None, :]
    picks = pick.shape[1]

    steps = peers.bit_length() - 2
    grows = width // GROUPS
    sizes = halves(grows, hid, steps)
    dma = pltpu.SemaphoreType.DMA
    vmem = pltpu.VMEM
    scratch = [
        vmem((2, rows, width), BF16),
        vmem((rows, rows + caps + hubs), BF16),
        vmem((rows, 1), F32),
        vmem((rows, picks), BF16),
        vmem((caps, width), BF16),
        vmem((caps, width), BF16),
        vmem((4, width), F32),
        vmem((peers // QUAD, 4, width), F32),
        vmem((QUAD, peers, width), BF16),
        vmem((rows, hid), F32),
        vmem((rows, hid), BF16),
        vmem((rows, width), BF16),
        vmem((rows, width), F32),
        vmem((caps, width), BF16),
        vmem((caps, width), BF16),
        vmem((peers // QUAD, 4, width), F32),
        vmem((peers // QUAD, 4, width), F32),
        vmem((GROUPS, grows, hid), BF16),
        vmem((GROUPS, grows, hid), BF16),
        vmem((GROUPS, grows, hid), F32),
        vmem(w_self.shape, BF16),
        vmem(w_neigh.shape, BF16),
        vmem(tile_weights.shape, tile_weights.dtype),
        vmem(cotangent.shape, BF16),
        vmem((QUAD, peers, width), BF16),
        vmem((QUAD, peers, width), BF16),
    ]
    scratch += [vmem((GROUPS, *sizes[s + 1]), BF16) for s in range(steps)] * 2
    q = len(offsets)
    far = peers // QUAD
    scratch += [
        dma((q,)), dma((q,)), dma((far,)), dma((far,)), dma((q,)), dma((q,)), dma((far,)), dma((far,)),
        dma((GROUPS,)), dma((GROUPS,)), dma((steps, GROUPS)), dma((steps, GROUPS)),
        dma((steps, GROUPS)), dma((steps, GROUPS)), dma((GROUPS,)), dma((GROUPS,)),
        dma((5,)), dma((QUAD,)), dma((QUAD,)), dma((QUAD,)), dma((QUAD,)),
    ]
    whole = pl.BlockSpec(memory_space=pltpu.VMEM)
    anywhere = pl.BlockSpec(memory_space=pl.ANY)
    out_rows, grad, both = pl.pallas_call(
        functools.partial(layer, peers, offsets, sizes),
        out_shape=(
            jax.ShapeDtypeStruct((rows, hid), BF16),
            jax.ShapeDtypeStruct((rows, width), BF16),
            jax.ShapeDtypeStruct((2, width, hid), BF16),
        ),
        in_specs=[pl.BlockSpec(memory_space=pltpu.SMEM)] + [anywhere] * 4 + [whole] * 2 + [anywhere],
        out_specs=(whole,) * 3,
        scratch_shapes=scratch,
        compiler_params=pltpu.CompilerParams(
            collective_id=0, has_side_effects=True, vmem_limit_bytes=56 * 1024 * 1024
        ),
        cost_estimate=pl.CostEstimate(
            flops=8 * 2 * rows * width * hid, bytes_accessed=16 * rows * width * 2, transcendentals=rows * hid
        ),
    )(tile_cols, features, w_self, w_neigh, tile_weights, pick, readers, cotangent)
    return out_rows, grad, both[0].astype(F32), both[1].astype(F32)


def solution(mesh):
    peers = mesh.shape["dom"]
    return jax.shard_map(
        functools.partial(on_device, peers),
        mesh=mesh,
        in_specs=(
            P("dom", None),
            P(),
            P(),
            P("dom", None),
            P("dom", None, None, None),
            P("dom", None, None),
            P("dom", None),
            P("dom", None),
            P("dom", None),
            P("dom", None),
        ),
        out_specs=(P("dom", None), P("dom", None), P(), P()),
        check_vma=False,
    )
```

```python
import functools

import jax
import jax.numpy as jnp
from jax import lax
from jax.experimental import pallas as pl
from jax.experimental.pallas import tpu as pltpu
from jax.sharding import PartitionSpec as P

REACH = 4
MESH = pl.DeviceIdType.MESH
F32 = jnp.float32
BF16 = jnp.bfloat16
GROUPS = 6
QUAD = 4


def near_offsets(reach):
    return list(range(1, reach + 1)) + [-distance for distance in range(1, reach + 1)]


def bit_orders(peers):
    bits = list(range(1, peers.bit_length() - 1))
    head, tail = bits[:-1], bits[-1:]
    orders = []
    for group in range(GROUPS):
        turn = (group % 3) * len(head) // 3
        order = head[turn:] + head[:turn]
        if group >= 3:
            order = order[:1] + order[:0:-1]
        orders.append(order + tail)
    return orders


def halves(rows, cols, steps):
    sizes = [(rows, cols)]
    for _ in range(steps):
        rows, cols = (rows // 2, cols) if rows > 16 else (rows, cols // 2)
        sizes.append((rows, cols))
    return sizes


def dot(left, right, dims=((1,), (0,))):
    return lax.dot_general(left, right, (dims, ((), ())), preferred_element_type=F32)


def layer(peers, offsets, sizes, cols_ref, count_ref, hubrow_ref, feat_hbm, ws_hbm, wn_hbm, tiles_hbm, sends_ref,
          flag_ref, cot_hbm,
          out_hbm, gfeat_ref, res_hbm, *scratch):
    steps = len(sizes) - 1
    (x, adj, inv, scat, going, halo, hub_out, hub_in, hub_all, pre, dpre, dneigh, own, back_out, back,
     hback_out, hback, core_out, core_in, acc, ws_ref, wn_ref, tiles_ref, cot_ref, fold_out, fold_in,
     pick_ref, out_ref, res_ref) = scratch[:29]
    rs_out, rs_in = scratch[29:29 + steps], scratch[29 + steps:29 + 2 * steps]
    (halo_s, halo_r, hub_s, hub_r, back_s, back_r, hback_s, hback_r, core_s, core_r, rs_s, rs_r,
     ag_s, ag_r, last_s, last_r, load_s, quad_s, quad_r, fold_s, fold_r, store_s) = scratch[29 + 2 * steps:]
    feat_ref = x.at[0]
    loads = [
        pltpu.make_async_copy(source, target, load_s.at[i])
        for i, (source, target) in enumerate(
            [(feat_hbm, feat_ref), (tiles_hbm, tiles_ref), (ws_hbm, ws_ref), (wn_hbm, wn_ref), (cot_hbm, cot_ref)]
        )
    ]
    for load in loads:
        load.start()
    seat = lax.axis_index("dom") % QUAD
    far = peers // QUAD
    me = lax.axis_index("dom")
    core = me % 2
    mate = me + 1 - 2 * core
    rows, width = x.shape[1:]
    hid = ws_ref.shape[1]
    row_blocks, slots, tile, _ = tiles_ref.shape
    col_blocks = adj.shape[1] // tile
    caps = halo.shape[0]
    orders = bit_orders(peers)
    grows = width // GROUPS

    def remote(src, dst, send, recv, peer):
        return pltpu.make_async_remote_copy(
            src_ref=src, dst_ref=dst, send_sem=send, recv_sem=recv, device_id=(peer,), device_id_type=MESH
        )

    barrier = pltpu.get_barrier_semaphore()

    def greet(k, carry):
        pl.semaphore_signal(barrier, inc=1, device_id=(lax.rem(me + k, peers),), device_id_type=MESH)
        return carry

    lax.fori_loop(1, peers, greet, 0)

    picks = pick_ref.shape[1]
    cap = sends_ref.shape[2]
    for q, offset in enumerate(offsets):
        peer = lax.rem(me + offset + peers, peers)
        live = lax.broadcasted_iota(jnp.int32, (1, cap), 1) < count_ref[0, peer]
        pick_ref[:, q * cap:(q + 1) * cap] = jnp.where(live, sends_ref[0, pl.ds(peer, 1), :], -1)
    lane = lax.broadcasted_iota(jnp.int32, (1, picks - caps), 1)
    extra = jnp.full((1, picks - caps), -1, jnp.int32)
    for i in range(4):
        extra = jnp.where((lane == i) | (lane == i + 4), hubrow_ref[0, i], extra)
    pick_ref[:, caps:] = extra
    scat[...] = (lax.broadcasted_iota(jnp.int32, (rows, picks), 0) == pick_ref[...]).astype(F32).astype(BF16)
    loads[0].wait()
    picked = dot(scat[...], feat_ref[...], ((0,), (0,)))
    going[...] = picked[:caps].astype(BF16)
    hub_out[...] = picked[caps:caps + 4]
    hub_in[me // QUAD] = picked[caps:caps + 4]
    pl.semaphore_wait(barrier, peers - 1)

    part = caps // len(offsets)

    def halo_copy(q):
        piece = pl.ds(q * part, part)
        return remote(going.at[piece], halo.at[piece], halo_s.at[q], halo_r.at[q],
                      lax.rem(me + offsets[q] + peers, peers))

    def hub_copy(k):
        return remote(hub_out, hub_in.at[me // QUAD], hub_s.at[k], hub_r.at[k], lax.rem(me + QUAD * k, peers))

    def mate_of(k):
        return me - seat + (seat + k) % QUAD

    def quad_copy(k):
        return remote(hub_all.at[seat], hub_all.at[seat], quad_s.at[k], quad_r.at[k], mate_of(k))

    def fold_copy(k):
        return remote(fold_out.at[(seat + k) % QUAD], fold_in.at[seat], fold_s.at[k], fold_r.at[k], mate_of(k))

    def back_copy(q):
        piece = pl.ds(q * part, part)
        return remote(back_out.at[piece], back.at[piece], back_s.at[q], back_r.at[q],
                      lax.rem(me - offsets[q] + peers, peers))

    def hback_copy(k):
        peer = lax.rem(me + QUAD * k, peers)
        return remote(hback_out.at[peer // QUAD], hback.at[me // QUAD], hback_s.at[k], hback_r.at[k], peer)

    def start_all(make):
        def body(k, carry):
            make(k).start()
            return carry
        lax.fori_loop(1, far, body, 0)

    def wait_recv_all(make):
        def body(k, carry):
            make(k).wait_recv()
            return carry
        lax.fori_loop(1, far, body, 0)

    def wait_send_all(make):
        def body(k, carry):
            make(k).wait_send()
            return carry
        lax.fori_loop(1, far, body, 0)

    start_all(hub_copy)
    for q in range(len(offsets)):
        halo_copy(q).start()

    def build(b, carry):
        weights = [tiles_ref[b, k].astype(F32) for k in range(slots)]
        at = pl.ds(pl.multiple_of(b * tile, tile), tile)
        inv[at, :] = 1.0 / (jnp.sum(sum(weights), axis=1, keepdims=True) + 1.0)
        for t in range(col_blocks):
            total = jnp.zeros((tile, tile), F32)
            for k in range(slots):
                total = total + weights[k] * (cols_ref[b, k] == t).astype(F32)
            if t * tile >= rows + caps:
                first = t * tile - rows - caps
                total = total * flag_ref[:, first:first + tile].astype(F32)
            adj[at, t * tile:(t + 1) * tile] = total.astype(BF16)
        return carry

    loads[1].wait()
    lax.fori_loop(0, row_blocks, build, 0)
    hubs = peers * 4
    made = lax.broadcasted_iota(jnp.int32, (hubs, hubs), 0)
    wanted = (made // 4) % QUAD * peers + made // (4 * QUAD) * 4 + made % 4
    turned = (lax.broadcasted_iota(jnp.int32, (hubs, hubs), 1) == wanted).astype(F32).astype(BF16)
    adj[:, rows + caps:] = dot(adj[:, rows + caps:], turned).astype(BF16)
    wait_recv_all(hub_copy)
    hub_all[seat] = jnp.concatenate([hub_in[j] for j in range(far)], axis=0).astype(BF16)
    for k in range(1, QUAD):
        quad_copy(k).start()
    loads[2].wait()
    half = rows // 2
    for r in range(2):
        at = slice(r * half, (r + 1) * half)
        own[at] = dot(adj[at, :rows], feat_ref[...])
        pre[at] = dot(feat_ref[at], ws_ref[...])

    for q in range(len(offsets)):
        halo_copy(q).wait_recv()
    for k in range(1, QUAD):
        quad_copy(k).wait_recv()
    loads[3].wait()
    loads[4].wait()

    for r in range(2):
        at = slice(r * half, (r + 1) * half)
        total = own[at] + dot(adj[at, rows:rows + caps], halo[...]) + dot(adj[at, rows + caps:], hub_all[...].reshape(hubs, width))
        neigh = (total * inv[at]).astype(BF16)
        x[1, at] = neigh
        whole = pre[at] + dot(neigh, wn_ref[...])
        sigma = jax.nn.sigmoid(whole)
        out_ref[at] = (whole * sigma).astype(BF16)
        dpre[at] = (cot_ref[at].astype(F32) * sigma * (1.0 + whole * (1.0 - sigma))).astype(BF16)

    out_store = pltpu.make_async_copy(out_ref, out_hbm, store_s.at[2 * GROUPS])
    out_store.start()

    def core_copy(g):
        return remote(core_out.at[g], core_in.at[g], core_s.at[g], core_r.at[g], mate)

    for g in range(0, GROUPS, 2):
        term = dot(x[1 - core, :, g * grows:(g + 2) * grows], dpre[...], ((0,), (0,))).astype(BF16)
        for i in range(2):
            core_out[g + i] = term[i * grows:(i + 1) * grows]
            core_copy(g + i).start()
    for g in range(0, GROUPS, 2):
        term = dot(x[core, :, g * grows:(g + 2) * grows], dpre[...], ((0,), (0,)))
        for i in range(2):
            acc[g + i] = term[i * grows:(i + 1) * grows]

    zero = me * 0
    places = [(zero, zero)] * GROUPS
    trail = [[None] * steps for _ in range(GROUPS)]

    def ds(row, col, size):
        unit = min(size[0], grows)
        return (pl.ds(pl.multiple_of(row, 16), unit), pl.ds(pl.multiple_of(col, 128), size[1]))

    def rs_copy(s, g):
        step = 2 ** orders[g][s]
        bit = (me // step) % 2
        return remote(rs_out[s].at[g], rs_in[s].at[g], rs_s.at[s, g], rs_r.at[s, g], me + step - 2 * step * bit)

    def rs_start(s, g):
        row, col = places[g]
        size = sizes[s + 1]
        bit = (me // 2 ** orders[g][s]) % 2
        if size[0] != sizes[s][0]:
            keep, give = (row + bit * size[0], col), (row + (1 - bit) * size[0], col)
        else:
            keep, give = (row, col + bit * size[1]), (row, col + (1 - bit) * size[1])
        rs_out[s][g] = acc[(g, *ds(*give, size))].astype(BF16)
        rs_copy(s, g).start()
        places[g] = keep

    def rs_end(s, g):
        rs_copy(s, g).wait_recv()
        spot = (g, *ds(*places[g], sizes[s + 1]))
        acc[spot] = acc[spot] + rs_in[s][g].astype(F32)

    def ag_place(s, g):
        row, col = zero, zero
        for t in range(s + 1):
            bit = (me // 2 ** orders[g][t]) % 2
            if sizes[t + 1][0] != sizes[t][0]:
                row = row + bit * sizes[t + 1][0]
            else:
                col = col + bit * sizes[t + 1][1]
        return row, col

    def ag_copy(s, g):
        step = 2 ** orders[g][s]
        bit = (me // step) % 2
        row, col = ag_place(s, g)
        size = sizes[s + 1]
        spot = res_ref.at[(core, *ds(row + g * grows, col, size))]
        return remote(spot, spot, ag_s.at[s, g], ag_r.at[s, g], me + step - 2 * step * bit)

    def store(side, g):
        spot = (core if side == 0 else 1 - core, pl.ds(g * grows, grows))
        return pltpu.make_async_copy(res_ref.at[spot], res_hbm.at[spot], store_s.at[side * GROUPS + g])

    def last_copy(g):
        spot = res_ref.at[core, pl.ds(g * grows, grows)]
        return remote(spot, spot, last_s.at[g], last_r.at[g], mate)

    for g in range(GROUPS):
        core_copy(g).wait_recv()
        acc[g] = acc[g] + core_in[g].astype(F32)
        rs_start(0, g)

    for r in range(2):
        at = slice(r * half, (r + 1) * half)
        dneigh[at] = (dot(dpre[at], wn_ref[...], ((1,), (1,))) * inv[at]).astype(BF16)
    back_out[...] = dot(adj[:, rows:rows + caps], dneigh[...], ((0,), (0,))).astype(BF16)
    for q in range(len(offsets)):
        back_copy(q).start()
    fold_out[...] = dot(adj[:, rows + caps:], dneigh[...], ((0,), (0,))).astype(BF16).reshape(QUAD, peers, width)
    fold_in[seat] = fold_out[seat]
    for k in range(1, QUAD):
        fold_copy(k).start()

    for s in range(steps):
        for g in range(GROUPS):
            rs_end(s, g)
            if s + 1 < steps:
                rs_start(s + 1, g)
            else:
                spot = ds(places[g][0] + g * grows, places[g][1], sizes[steps])
                res_ref[(core, *spot)] = acc[(g, *ds(*places[g], sizes[steps]))].astype(BF16)
                ag_copy(steps - 1, g).start()
        if s == 0:
            for r in range(2):
                at = slice(r * half, (r + 1) * half)
                own[at] = dot(dpre[at], ws_ref[...], ((1,), (1,)))
        elif s == 1:
            own[...] += dot(adj[:, :rows], dneigh[...], ((0,), (0,)))
            for k in range(1, QUAD):
                fold_copy(k).wait_recv()
            fold = jnp.sum(fold_in[...].astype(F32), axis=0)
            for j in range(far):
                hback_out[j] = fold[4 * j:4 * j + 4]
            hback[me // QUAD] = hback_out[me // QUAD]
            start_all(hback_copy)

    for s in reversed(range(steps)):
        for g in range(GROUPS):
            ag_copy(s, g).wait_recv()
            if s > 0:
                ag_copy(s - 1, g).start()
            else:
                last_copy(g).start()
                store(0, g).start()

    for q in range(len(offsets)):
        back_copy(q).wait_recv()
    wait_recv_all(hback_copy)
    hub_sum = jnp.sum(hback[...], axis=0)
    coarse = hub_sum.astype(BF16).astype(F32)
    hub_part = jnp.concatenate(
        [coarse, hub_sum - coarse, jnp.zeros((picks - caps - 8, width), F32)], axis=0
    ).astype(BF16)
    for r in range(2):
        at = slice(r * half, (r + 1) * half)
        total = own[at] + dot(scat[at, :caps], back[...]) + dot(scat[at, caps:], hub_part)
        gfeat_ref[at] = total.astype(BF16)

    for g in range(GROUPS):
        last_copy(g).wait_recv()
        store(1, g).start()
    out_store.wait()
    for q in range(len(offsets)):
        halo_copy(q).wait_send()
        back_copy(q).wait_send()
    for k in range(1, QUAD):
        quad_copy(k).wait_send()
        fold_copy(k).wait_send()
    wait_send_all(hub_copy)
    wait_send_all(hback_copy)
    for g in range(GROUPS):
        core_copy(g).wait_send()
        store(0, g).wait()
        store(1, g).wait()
        last_copy(g).wait_send()
        for s in range(steps):
            rs_copy(s, g).wait_send()
            ag_copy(s, g).wait_send()


def on_device(peers, features, w_self, w_neigh, tile_cols, tile_weights, send_rows, send_counts, hub_rows, readers,
              cotangent):
    rows, width = features.shape
    hid = w_self.shape[1]
    cap = send_rows.shape[2]
    offsets = near_offsets(REACH)
    caps = len(offsets) * cap
    hubs = readers.shape[1]
    tile = tile_weights.shape[2]
    picks = caps + tile

    steps = peers.bit_length() - 2
    grows = width // GROUPS
    sizes = halves(grows, hid, steps)
    dma = pltpu.SemaphoreType.DMA
    vmem = pltpu.VMEM
    scratch = [
        vmem((2, rows, width), BF16),
        vmem((rows, rows + caps + hubs), BF16),
        vmem((rows, 1), F32),
        vmem((rows, picks), BF16),
        vmem((caps, width), BF16),
        vmem((caps, width), BF16),
        vmem((4, width), F32),
        vmem((peers // QUAD, 4, width), F32),
        vmem((QUAD, peers, width), BF16),
        vmem((rows, hid), F32),
        vmem((rows, hid), BF16),
        vmem((rows, width), BF16),
        vmem((rows, width), F32),
        vmem((caps, width), BF16),
        vmem((caps, width), BF16),
        vmem((peers // QUAD, 4, width), F32),
        vmem((peers // QUAD, 4, width), F32),
        vmem((GROUPS, grows, hid), BF16),
        vmem((GROUPS, grows, hid), BF16),
        vmem((GROUPS, grows, hid), F32),
        vmem(w_self.shape, BF16),
        vmem(w_neigh.shape, BF16),
        vmem(tile_weights.shape, tile_weights.dtype),
        vmem(cotangent.shape, BF16),
        vmem((QUAD, peers, width), BF16),
        vmem((QUAD, peers, width), BF16),
        vmem((1, picks), jnp.int32),
        vmem((rows, hid), BF16),
        vmem((2, width, hid), BF16),
    ]
    scratch += [vmem((GROUPS, *sizes[s + 1]), BF16) for s in range(steps)] * 2
    q = len(offsets)
    far = peers // QUAD
    scratch += [
        dma((q,)), dma((q,)), dma((far,)), dma((far,)), dma((q,)), dma((q,)), dma((far,)), dma((far,)),
        dma((GROUPS,)), dma((GROUPS,)), dma((steps, GROUPS)), dma((steps, GROUPS)),
        dma((steps, GROUPS)), dma((steps, GROUPS)), dma((GROUPS,)), dma((GROUPS,)),
        dma((5,)), dma((QUAD,)), dma((QUAD,)), dma((QUAD,)), dma((QUAD,)), dma((2 * GROUPS + 1,)),
    ]
    whole = pl.BlockSpec(memory_space=pltpu.VMEM)
    anywhere = pl.BlockSpec(memory_space=pltpu.HBM)
    out_rows, grad, both = pl.pallas_call(
        functools.partial(layer, peers, offsets, sizes),
        out_shape=(
            jax.ShapeDtypeStruct((rows, hid), BF16),
            jax.ShapeDtypeStruct((rows, width), BF16),
            jax.ShapeDtypeStruct((2, width, hid), BF16),
        ),
        in_specs=[pl.BlockSpec(memory_space=pltpu.SMEM)] * 3 + [anywhere] * 4 + [whole] * 2 + [anywhere],
        out_specs=(anywhere, whole, anywhere),
        scratch_shapes=scratch,
        compiler_params=pltpu.CompilerParams(
            collective_id=0, has_side_effects=True, vmem_limit_bytes=56 * 1024 * 1024
        ),
        cost_estimate=pl.CostEstimate(
            flops=8 * 2 * rows * width * hid, bytes_accessed=16 * rows * width * 2, transcendentals=rows * hid
        ),
    )(tile_cols, send_counts, hub_rows, features, w_self, w_neigh, tile_weights, send_rows, readers, cotangent)
    return out_rows, grad, both[0].astype(F32), both[1].astype(F32)


def solution(mesh):
    peers = mesh.shape["dom"]
    return jax.shard_map(
        functools.partial(on_device, peers),
        mesh=mesh,
        in_specs=(
            P("dom", None),
            P(),
            P(),
            P("dom", None),
            P("dom", None, None, None),
            P("dom", None, None),
            P("dom", None),
            P("dom", None),
            P("dom", None),
            P("dom", None),
        ),
        out_specs=(P("dom", None), P("dom", None), P(), P()),
        check_vma=False,
    )
```
